32 devices in a mesh: sect: 8 (over z, y), grp: 4 (over x, core).
Axes of the slice: x: 2, y: 2, z: 4, core: 2. Of those that a mesh axis runs over, the one named last changes fastest.
Arguments:
- volts: bfloat16 [384, 8192], P('sect', 'grp'), may hold values from -6 to 6
- pfb_window: float32 [4, 512], replicated, may hold values from -3 to 3
- chan_order: int32 [256], replicated, may hold values from 0 to 255, each once
- delays: float32 [128, 384], replicated, may hold values from -2 to 2
- antenna_map: int32 [384], replicated, may hold values from 0 to 383, each once
- pointing: int32 [320], P('sect'), may hold values from 0 to 127
Outputs:
- vis: float32 [256, 2, 384, 384], P('grp', None, 'sect')
- beam_series: float32 [320, 16], P('sect', 'grp')
The draws below stay inside these ranges and needn't reach their ends.
Inputs may be any that keep to these rules, and one draw needn't show every extreme that they name: `chan_order`: each channel stands in exactly one slot. `antenna_map`: each delay column is named by exactly one input row.
All inputs are finite; a program needn't handle non-finite values.
Results may differ from the reference program's by a relative error of at most 0.0071.
Values may be sent and summed in bfloat16 or wider, within the bound.
A program may use at most 64 MiB of HBM per device.

```python
import math
import jax
import jax.numpy as jnp
from jax import lax

NCH = 256
TAPS = 4
NPOINT = 128
NI = 384
SPEC = 16
NBEAM = 320


def place_ends(drawn, rng, least, largest):
    longest = drawn.shape.index(max(drawn.shape))
    spots = []
    for shift in (0, 1):
        where = [jax.random.randint(jax.random.fold_in(rng, axis), (), 0, length) for axis, length in enumerate(drawn.shape)]
        where[longest] = (where[longest] + shift) % drawn.shape[longest]
        spots.append(tuple(where))
    return drawn.at[spots[0]].set(least).at[spots[1]].set(largest)


def block_scale(rng, shape, cuts, least, high):
    gain = 1.0
    for dim, blocks in cuts:
        draws = jax.random.uniform(jax.random.fold_in(jax.random.fold_in(rng, 6), dim), (blocks,), jnp.float32, least / len(cuts), high / len(cuts))
        gain = gain * jnp.repeat(jnp.exp(draws), shape[dim] // blocks).reshape((-1,) + (1,) * (len(shape) - 1 - dim))
    return gain


def normal_values(stream_key, dims, spread, limit, split=(), kind=jnp.bfloat16):
    level = block_scale(stream_key, dims, split, -0.22, 0.18) if split else 1.0
    values = jax.random.normal(stream_key, dims, jnp.float32) * spread * level
    return jnp.minimum(jnp.maximum(values, -limit), limit).astype(kind)


def setup_inputs(seed: int = 0) -> dict:
    key_of = jax.random.split(jax.random.key(seed), 7)
    return {
        "volts": normal_values(key_of[0], (NI, SPEC * 2 * NCH), 1.0, 6.0, ((0, 8), (1, 4))),
        "pfb_window": normal_values(key_of[1], (TAPS, 2 * NCH), 0.5, 3.0, (), jnp.float32),
        "chan_order": jax.random.permutation(key_of[2], NCH).astype(jnp.int32),
        "delays": jnp.clip(jax.random.uniform(key_of[3], (NPOINT, NI), jnp.float32, -2.0, 2.0), -2.0, 2.0),
        "antenna_map": jax.random.permutation(key_of[4], NI).astype(jnp.int32),
        "pointing": place_ends(jax.random.randint(key_of[5], (NBEAM,), 0, NPOINT), jax.random.fold_in(key_of[5], 1), 0, NPOINT - 1).astype(jnp.int32),
    }


def dft_matrix(chan_order, frame_len):
    samples = jnp.arange(frame_len, dtype=jnp.int32)
    product = samples[:, None] * chan_order[None, :].astype(jnp.int32) % frame_len
    angles = product.astype(jnp.float32) * (2.0 * math.pi / frame_len)
    scaled = 1.0 / math.sqrt(frame_len)
    return (jnp.stack([jnp.cos(angles), -jnp.sin(angles)], axis=1) * scaled).astype(jnp.bfloat16)

def steering(delays, antenna_map, pointing, channels):
    chosen = jnp.take(delays, pointing, axis=0)
    chosen = jnp.take(chosen, antenna_map, axis=1)
    turns = (channels.astype(jnp.float32) + 0.5) * (2.0 * math.pi / NCH)
    phases = chosen[None, :, :] * turns[:, None, None]
    width_scale = 1.0 / math.sqrt(delays.shape[1])
    return (jnp.stack([jnp.cos(phases), -jnp.sin(phases)], axis=1) * width_scale).astype(jnp.bfloat16)

def reference(volts, pfb_window, chan_order, delays, antenna_map, pointing):
    frame_len = 2 * NCH
    frames = volts.reshape(NI, SPEC, frame_len).astype(jnp.float32)
    padded = jnp.concatenate([jnp.zeros((NI, TAPS - 1, frame_len), jnp.float32), frames], axis=1)
    filtered = jnp.zeros((NI, SPEC, frame_len), jnp.float32)
    for tap_index in range(TAPS):
        begin = TAPS - 1 - tap_index
        filtered = filtered + pfb_window[tap_index][None, None, :] * padded[:, begin:begin + SPEC]
    filtered = filtered.astype(jnp.bfloat16)
    dft_table = dft_matrix(chan_order, frame_len)
    spectra = jnp.einsum('isn,npk->kpsi', filtered.astype(jnp.float32), dft_table.astype(jnp.float32)).astype(jnp.bfloat16)
    gram_scale = 1.0 / SPEC

    def one_channel(inputs):
        data, channel = inputs
        flat = data.reshape(2 * SPEC, NI).astype(jnp.float32)
        swapped = jnp.concatenate([data[1], -data[0]], axis=0).astype(jnp.float32)
        real_part = jnp.dot(flat.T, flat, preferred_element_type=jnp.float32)
        imag_part = jnp.dot(swapped.T, flat, preferred_element_type=jnp.float32)
        block = jnp.stack([real_part, imag_part], axis=0) * gram_scale
        weights = steering(delays, antenna_map, pointing, channel[None])[0].astype(jnp.float32)
        values = data.astype(jnp.float32)
        from_real = jnp.einsum('bj,stj->sbt', weights[0], values)
        from_imag = jnp.einsum('bj,stj->sbt', weights[1], values)
        beam_real = from_real[0] - from_imag[1]
        beam_imag = from_real[1] + from_imag[0]
        return (block, beam_real * beam_real + beam_imag * beam_imag)
    vis, beam_power = lax.map(one_channel, (spectra, chan_order))
    beam_series = lax.optimization_barrier(jnp.sum(beam_power, axis=0)) * (1.0 / math.sqrt(NCH))
    return (vis, beam_series)
```

```python
import functools
import math

import jax
import jax.numpy as jnp
import numpy as np
from jax import lax
from jax.experimental import pallas as pl
from jax.experimental.pallas import tpu as pltpu
from jax.sharding import PartitionSpec as P

NCH = 256
TAPS = 4
FRAME = 2 * NCH
BLOCK = 512
MESH = pl.DeviceIdType.MESH


def round_up(n, m):
    return -(-n // m) * m


def cos_fit(degree):
    nodes = 0.125 + 0.125 * np.cos(np.pi * (np.arange(64) + 0.5) / 64)
    fit = np.polynomial.chebyshev.Chebyshev.fit(
        nodes, np.cos(2 * np.pi * np.sqrt(nodes)), degree, domain=[0.0, 0.25]
    )
    return [float(c) for c in fit.convert(kind=np.polynomial.Polynomial).coef]


COS = cos_fit(6)


def cos_turns(u, scale):
    r = u - jnp.round(u)
    y = r * r
    total = jnp.full_like(y, COS[-1] * scale)
    for c in COS[-2::-1]:
        total = total * y + c * scale
    return total


def dot(a, b, dims=((1,), (0,))):
    return lax.dot_general(a, b, (dims, ((), ())), preferred_element_type=jnp.float32)


def pieces(x):
    hi = x.astype(jnp.bfloat16)
    rest = x - hi.astype(jnp.float32)
    mid = rest.astype(jnp.bfloat16)
    low = (rest - mid.astype(jnp.float32)).astype(jnp.bfloat16)
    return hi, mid, low


def one_hot(rows, cols):
    return jnp.where(rows == cols, 1.0, 0.0).astype(jnp.bfloat16)


def iota(shape, dim):
    return lax.broadcasted_iota(jnp.int32, shape, dim)


def gather_kernel(
    dims,
    volts, pfb, chan_row, chan, delays, amap, pointing,
    gathered, series,
    halo, table, place, merge, turns, weights, sent, got, spec, power,
    halo_sem, turn_send, turn_recv, far_send, far_recv, near_send, near_recv,
    beam_send, beam_recv, out_sem,
):
    ns, ng, slots, here, th, inputs, beams = dims
    total = th * ng
    lanes_g = round_up(2 * slots, 128)
    chunk = sent.shape[2]
    blocks = NCH * 2 * th // BLOCK
    per_block = BLOCK // (2 * total)
    width = max(128, 2 * total)
    per_tile = width // (2 * total)
    tiles = BLOCK // width
    brows = turns.shape[0]
    inner = 2 if ns % 2 == 0 else 1
    outer = ns // inner

    sect = lax.axis_index("sect")
    grp = lax.axis_index("grp")
    row = sect // inner
    col = sect % inner

    def grp_peer(d):
        return lax.rem(grp + d, ng)

    def far_peer(d):
        return lax.rem(row + d, outer)

    barrier = pltpu.get_barrier_semaphore()
    for d in range(1, ng):
        pl.semaphore_signal(barrier, inc=1, device_id=(sect, grp_peer(d)), device_id_type=MESH)
    for d in range(1, outer):
        pl.semaphore_signal(
            barrier, inc=1, device_id=(far_peer(d) * inner + col, grp), device_id_type=MESH
        )
    if inner == 2:
        pl.semaphore_signal(
            barrier, inc=1, device_id=(row * inner + 1 - col, grp), device_id_type=MESH
        )

    def rows_of(s):
        return pl.ds(pl.multiple_of(s * here, 16), here)

    pl.semaphore_wait(barrier, (ng - 1) + (outer - 1) + (inner - 1))

    keep = TAPS - 1
    halo_copy = pltpu.make_async_remote_copy(
        src_ref=volts.at[:, (th - keep) * FRAME :],
        dst_ref=halo,
        send_sem=halo_sem.at[0],
        recv_sem=halo_sem.at[1],
        device_id=(sect, lax.rem(grp + 1, ng)),
        device_id_type=MESH,
    )

    @pl.when(grp < ng - 1)
    def _():
        halo_copy.start()

    columns = ng * lanes_g
    c = iota((NCH, columns), 1)
    slot = jnp.where(
        c % lanes_g < 2 * slots, (c // lanes_g) * slots + (c % lanes_g) // 2, -1
    )
    expand = one_hot(iota((NCH, columns), 0), slot)
    chan8 = jnp.broadcast_to(chan_row[...].astype(jnp.float32), (8, NCH)).astype(jnp.bfloat16)
    chan_cols = dot(chan8, expand)[0:1, :]
    step = 128
    quarter = (iota((1, columns), 1) % 2).astype(jnp.float32) * 0.25
    for begin in range(0, FRAME, step):
        n = (iota((step, columns), 0) + begin).astype(jnp.float32)
        angle = n * chan_cols * (1.0 / FRAME) + quarter
        table[begin : begin + step, :] = cos_turns(angle, 1.0 / math.sqrt(FRAME)).astype(
            jnp.bfloat16
        )

    k = iota((th * lanes_g, chunk), 0)
    c = iota((th * lanes_g, chunk), 1)
    place[...] = one_hot(k, (c % th) * lanes_g + c // th)

    need = per_block * 2 * th
    span = need if need % 128 == 0 else chunk

    def merge_matrix(offset):
        k = iota((ng * span, BLOCK), 0)
        c = iota((ng * span, BLOCK), 1)
        return one_hot(k, ((c % total) // th) * span + (c // total) * th + c % th + offset)

    if span == need:
        merge[...] = merge_matrix(0)

    @pl.when(grp == 0)
    def _():
        halo[...] = jnp.zeros_like(halo)

    @pl.when(grp > 0)
    def _():
        halo_copy.wait_recv()

    frames = [halo[:, i * FRAME : (i + 1) * FRAME].astype(jnp.float32) for i in range(keep)]
    frames += [volts[:, i * FRAME : (i + 1) * FRAME].astype(jnp.float32) for i in range(th)]
    filtered = []
    for t in range(th):
        value = pfb[0:1, :] * frames[t + keep]
        for tap in range(1, TAPS):
            value = value + pfb[tap : tap + 1, :] * frames[t + keep - tap]
        filtered.append(value.astype(jnp.bfloat16))
    filtered = jnp.concatenate(filtered, axis=0)
    made = dot(filtered, table[...]).astype(jnp.bfloat16)
    for g in range(ng):
        flat = jnp.concatenate(
            [
                made[t * here : (t + 1) * here, g * lanes_g : (g + 1) * lanes_g]
                for t in range(th)
            ],
            axis=1,
        )
        sent[g] = dot(flat, place[...]).astype(jnp.bfloat16)

    turn_copies = []
    for d in range(1, ng):
        peer = grp_peer(d)
        copy = pltpu.make_async_remote_copy(
            src_ref=sent.at[peer],
            dst_ref=got.at[grp],
            send_sem=turn_send.at[d],
            recv_sem=turn_recv.at[d],
            device_id=(sect, peer),
            device_id_type=MESH,
        )
        copy.start()
        turn_copies.append(copy)
    got[grp] = sent[grp]

    b = beams
    eye = iota((b, b), 0) == iota((b, b), 1)
    spread = jnp.broadcast_to(pointing[...].astype(jnp.float32), (b, b))
    point_col = jnp.sum(jnp.where(eye, spread, 0.0), axis=1, keepdims=True).astype(jnp.int32)
    points = delays.shape[0]
    pick = one_hot(iota((b, points), 1), jnp.broadcast_to(point_col, (b, points)))
    hi, mid, low = pieces(delays[...])
    chosen = (dot(pick, hi) + dot(pick, mid)) + dot(pick, low)
    order = one_hot(
        iota((inputs, inputs), 0), jnp.broadcast_to(amap[...], (inputs, inputs))
    )
    hi, mid, low = pieces(chosen)
    chosen = (dot(hi, order) + dot(mid, order)) + dot(low, order)
    turns[...] = jnp.zeros_like(turns)
    turns[0:b, :] = chosen * (1.0 / NCH)

    for copy in turn_copies:
        copy.wait_recv()

    mine = rows_of(sect)
    for q in range(blocks):
        begin = q * need if span == need else 0
        flat = jnp.concatenate(
            [got[g, :, begin : begin + span] for g in range(ng)], axis=1
        )
        matrix = merge[...] if span == need else merge_matrix(q * need)
        spec[q, mine, :] = dot(flat, matrix).astype(jnp.bfloat16)

    def far_copy(q, d):
        return pltpu.make_async_remote_copy(
            src_ref=spec.at[q, mine, :],
            dst_ref=spec.at[q, mine, :],
            send_sem=far_send.at[q, d],
            recv_sem=far_recv.at[q, d],
            device_id=(far_peer(d) * inner + col, grp),
            device_id_type=MESH,
        )

    def near_copy(q, d):
        begun = rows_of(lax.rem(row - d + outer, outer) * inner + col)
        return pltpu.make_async_remote_copy(
            src_ref=spec.at[q, begun, :],
            dst_ref=spec.at[q, begun, :],
            send_sem=near_send.at[q, d],
            recv_sem=near_recv.at[q, d],
            device_id=(row * inner + 1 - col, grp),
            device_id_type=MESH,
        )

    for q in range(blocks):
        for d in range(1, outer):
            far_copy(q, d).start()
        if inner == 2:
            near_copy(q, 0).start()

    scale = 1.0 / math.sqrt(inputs)

    def weigh(tile):
        for k in range(per_tile):
            channel = chan[grp * slots + tile * per_tile + k].astype(jnp.float32) + 0.5
            for part in range(2):
                at = (k * 2 + part) * brows
                weights[tile, at : at + brows, :] = cos_turns(
                    turns[...] * channel + 0.25 * part, scale
                ).astype(jnp.bfloat16)

    for q in range(blocks):
        pl.loop(q * tiles, (q + 1) * tiles)(weigh)
        for d in range(1, outer):
            far_copy(q, d).wait_recv()
            if inner == 2:
                near_copy(q, d).start()

    lane = iota((brows, width), 1)
    slot_in = lane // (2 * total)
    first = (lane // total) % 2 == 0
    out_copies = []
    power[ng] = jnp.zeros_like(power[ng])
    acc = jnp.zeros((brows, width), jnp.float32)
    for q in range(blocks):
        if inner == 2:
            for d in range(outer):
                near_copy(q, d).wait_recv()
        copy = pltpu.make_async_copy(spec.at[q], gathered.at[q], out_sem.at[q])
        copy.start()
        out_copies.append(copy)
        for i in range(tiles):
            data = spec[q, :, i * width : (i + 1) * width]
            mixed = dot(weights[q * tiles + i], data)
            both = []
            for part in range(2):
                picked = jnp.zeros((brows, width), jnp.float32)
                for k in range(per_tile):
                    at = (k * 2 + part) * brows
                    picked = jnp.where(slot_in == k, mixed[at : at + brows, :], picked)
                both.append(picked)
            forward = pltpu.roll(both[1], total, 1)
            backward = pltpu.roll(both[1], width - total, 1)
            beam = both[0] + jnp.where(first, -backward, forward)
            acc = acc + beam * beam
    shift = width // 2
    while shift >= total:
        acc = acc + pltpu.roll(acc, shift, 1)
        shift //= 2
    power[ng] = acc[:, : power.shape[2]]

    beam_copies = []
    for d in range(1, ng):
        copy = pltpu.make_async_remote_copy(
            src_ref=power.at[ng],
            dst_ref=power.at[d],
            send_sem=beam_send.at[d],
            recv_sem=beam_recv.at[d],
            device_id=(sect, grp_peer(d)),
            device_id_type=MESH,
        )
        copy.start()
        beam_copies.append(copy)
    for q in range(blocks):
        for d in range(1, outer):
            far_copy(q, d).wait_send()
        if inner == 2:
            for d in range(outer):
                near_copy(q, d).wait_send()
    for copy in turn_copies:
        copy.wait_send()

    @pl.when(grp < ng - 1)
    def _():
        halo_copy.wait_send()

    for copy in out_copies:
        copy.wait()
    summed = power[ng]
    for d, copy in enumerate(beam_copies):
        copy.wait_recv()
        summed = summed + power[d + 1]
    lanes = summed.shape[1]
    turned = pltpu.roll(summed, lax.rem(lanes - grp * th, lanes), 1)
    series[...] = turned[:beams, :th] * (1.0 / math.sqrt(NCH))
    for copy in beam_copies:
        copy.wait_send()


def vis_kernel(here, total, per_tile, tiles, spec, vis):
    width = spec.shape[2] // tiles
    mine = pl.ds(pl.multiple_of(lax.axis_index("sect") * here, 16), here)
    lane = iota((here, width), 1)
    slot_in = lane // (2 * total)
    first = (lane // total) % 2 == 0
    for i in range(tiles):
        cols = slice(i * width, (i + 1) * width)
        local = spec[0, mine, cols].astype(jnp.float32)
        forward = pltpu.roll(local, total, 1)
        backward = pltpu.roll(local, width - total, 1)
        swapped = jnp.where(first, backward, -forward)
        left = []
        for k in range(per_tile):
            for part in (local, swapped):
                left.append(jnp.where(slot_in == k, part, 0.0).astype(jnp.bfloat16))
        block = dot(jnp.concatenate(left, axis=0), spec[0, :, cols], ((1,), (1,)))
        block = block * (1.0 / total)
        for k in range(per_tile):
            for part in range(2):
                at = (k * 2 + part) * here
                vis[i * per_tile + k, part] = block[at : at + here, :]


def per_device(ns, ng, volts, pfb_window, chan_order, delays, antenna_map, pointing):
    here = volts.shape[0]
    th = volts.shape[1] // FRAME
    inputs = delays.shape[1]
    beams = pointing.shape[0]
    slots = NCH // ng
    total = th * ng
    brows = round_up(beams, 16)
    lanes_g = round_up(2 * slots, 128)
    chunk = round_up(2 * slots * th, 128)
    blocks = NCH * 2 * th // BLOCK
    width = max(128, 2 * total)
    per_tile = width // (2 * total)
    tiles = BLOCK // width
    need = BLOCK // (2 * total) * 2 * th
    span = need if need % 128 == 0 else chunk
    outer = ns // 2 if ns % 2 == 0 else ns
    bf16, f32 = jnp.bfloat16, jnp.float32
    vmem = pl.BlockSpec(memory_space=pltpu.VMEM)
    dims = (ns, ng, slots, here, th, inputs, beams)
    dma = pltpu.SemaphoreType.DMA
    gathered, series = pl.pallas_call(
        functools.partial(gather_kernel, dims),
        out_shape=(
            jax.ShapeDtypeStruct((blocks, inputs, BLOCK), bf16),
            jax.ShapeDtypeStruct((beams, th), f32),
        ),
        in_specs=[vmem, vmem, vmem, pl.BlockSpec(memory_space=pltpu.SMEM), vmem, vmem, vmem],
        out_specs=(pl.BlockSpec(memory_space=pl.ANY), vmem),
        scratch_shapes=[
            pltpu.VMEM((here, (TAPS - 1) * FRAME), bf16),
            pltpu.VMEM((FRAME, ng * lanes_g), bf16),
            pltpu.VMEM((th * lanes_g, chunk), bf16),
            pltpu.VMEM((ng * span, BLOCK), bf16),
            pltpu.VMEM((brows, inputs), f32),
            pltpu.VMEM((blocks * tiles, per_tile * 2 * brows, inputs), bf16),
            pltpu.VMEM((ng, here, chunk), bf16),
            pltpu.VMEM((ng, here, chunk), bf16),
            pltpu.VMEM((blocks, inputs, BLOCK), bf16),
            pltpu.VMEM((ng + 1, brows, round_up(total, 128)), f32),
            dma((2,)),
            dma((ng,)),
            dma((ng,)),
            dma((blocks, outer)),
            dma((blocks, outer)),
            dma((blocks, outer)),
            dma((blocks, outer)),
            dma((ng,)),
            dma((ng,)),
            dma((blocks,)),
        ],
        compiler_params=pltpu.CompilerParams(
            collective_id=0, has_side_effects=True, vmem_limit_bytes=48 * 1024 * 1024
        ),
    )(
        volts,
        pfb_window,
        chan_order.reshape(1, -1),
        chan_order,
        delays,
        antenna_map.reshape(1, -1),
        pointing.reshape(1, -1),
    )
    vis = pl.pallas_call(
        functools.partial(vis_kernel, here, total, per_tile, tiles),
        grid=(blocks,),
        out_shape=jax.ShapeDtypeStruct((slots, 2, here, inputs), f32),
        in_specs=[pl.BlockSpec((1, inputs, BLOCK), lambda q: (q, 0, 0))],
        out_specs=pl.BlockSpec(
            (slots // blocks, 2, here, inputs), lambda q: (q, 0, 0, 0)
        ),
        compiler_params=pltpu.CompilerParams(vmem_limit_bytes=48 * 1024 * 1024),
    )(gathered)
    return (vis, series)


def solution(mesh):
    ns, ng = mesh.shape["sect"], mesh.shape["grp"]
    return jax.shard_map(
        functools.partial(per_device, ns, ng),
        mesh=mesh,
        in_specs=(P("sect", "grp"), P(), P(), P(), P(), P("sect")),
        out_specs=(P("grp", None, "sect", None), P("sect", "grp")),
        check_vma=False,
    )
```

```python
import functools
import math

import jax
import jax.numpy as jnp
import numpy as np
from jax import lax
from jax.experimental import pallas as pl
from jax.experimental.pallas import tpu as pltpu
from jax.sharding import PartitionSpec as P

NCH = 256
TAPS = 4
FRAME = 2 * NCH
BLOCK = 512
MESH = pl.DeviceIdType.MESH


def round_up(n, m):
    return -(-n // m) * m


def cos_fit(degree):
    nodes = 0.125 + 0.125 * np.cos(np.pi * (np.arange(64) + 0.5) / 64)
    fit = np.polynomial.chebyshev.Chebyshev.fit(
        nodes, np.cos(2 * np.pi * np.sqrt(nodes)), degree, domain=[0.0, 0.25]
    )
    return [float(c) for c in fit.convert(kind=np.polynomial.Polynomial).coef]


COS = cos_fit(6)


def cos_turns(u, scale):
    r = u - jnp.round(u)
    y = r * r
    total = jnp.full_like(y, COS[-1] * scale)
    for c in COS[-2::-1]:
        total = total * y + c * scale
    return total


def dot(a, b, dims=((1,), (0,))):
    return lax.dot_general(a, b, (dims, ((), ())), preferred_element_type=jnp.float32)


def pieces(x):
    hi = x.astype(jnp.bfloat16)
    rest = x - hi.astype(jnp.float32)
    mid = rest.astype(jnp.bfloat16)
    low = (rest - mid.astype(jnp.float32)).astype(jnp.bfloat16)
    return hi, mid, low


def one_hot(rows, cols):
    return jnp.where(rows == cols, 1.0, 0.0).astype(jnp.bfloat16)


def iota(shape, dim):
    return lax.broadcasted_iota(jnp.int32, shape, dim)


def gather_kernel(
    dims,
    volts_in, pfb_in, chan_in, chan, delays_in, amap_in, pointing_in,
    gathered, series,
    volts, pfb, chan_row, delays, amap, pointing, in_sem,
    halo, table, place, merge, turns, weights, sent, got, spec, power,
    halo_sem, turn_send, turn_recv, line_send, line_recv, near_send, near_recv,
    extra_send, extra_recv, beam_send, beam_recv, out_sem,
):
    ns, ng, slots, here, th, inputs, beams = dims
    total = th * ng
    lanes_g = round_up(2 * slots, 128)
    chunk = sent.shape[2]
    blocks = NCH * 2 * th // BLOCK
    per_block = BLOCK // (2 * total)
    width = max(128, 2 * total)
    per_tile = width // (2 * total)
    tiles = BLOCK // width
    brows = turns.shape[0]
    inner = 2 if ns % 2 == 0 else 1
    outer = ns // inner

    sect = lax.axis_index("sect")
    grp = lax.axis_index("grp")
    row = sect // inner
    col = sect % inner

    def grp_peer(d):
        return lax.rem(grp + d, ng)

    barrier = pltpu.get_barrier_semaphore()
    for d in range(1, ng):
        pl.semaphore_signal(barrier, inc=1, device_id=(sect, grp_peer(d)), device_id_type=MESH)
    for way in (1, -1):

        @pl.when((row + way >= 0) & (row + way < outer))
        def _(way=way):
            pl.semaphore_signal(
                barrier, inc=1, device_id=((row + way) * inner + col, grp), device_id_type=MESH
            )

    if inner == 2:
        pl.semaphore_signal(
            barrier, inc=1, device_id=(row * inner + 1 - col, grp), device_id_type=MESH
        )

    loads = []
    operands = ((chan_in, chan_row.at[0]), (volts_in, volts), (pfb_in, pfb),
                (delays_in, delays), (amap_in, amap.at[0]), (pointing_in, pointing.at[0]))
    for at, (src, dst) in enumerate(operands):
        loads.append(pltpu.make_async_copy(src, dst, in_sem.at[at]))
        loads[-1].start()

    def rows_of(s):
        return pl.ds(pl.multiple_of(s * here, 16), here)

    k = iota((th * lanes_g, chunk), 0)
    c = iota((th * lanes_g, chunk), 1)
    place[...] = one_hot(k, (c % th) * lanes_g + c // th)

    in_line = (row > 0).astype(jnp.int32) + (row < outer - 1).astype(jnp.int32)
    pl.semaphore_wait(barrier, (ng - 1) + (inner - 1) + in_line)

    keep = TAPS - 1
    halo_copy = pltpu.make_async_remote_copy(
        src_ref=volts_in.at[:, (th - keep) * FRAME :],
        dst_ref=halo,
        send_sem=halo_sem.at[0],
        recv_sem=halo_sem.at[1],
        device_id=(sect, lax.rem(grp + 1, ng)),
        device_id_type=MESH,
    )

    @pl.when(grp < ng - 1)
    def _():
        halo_copy.start()

    loads[0].wait()
    columns = ng * lanes_g
    c = iota((NCH, columns), 1)
    slot = jnp.where(
        c % lanes_g < 2 * slots, (c // lanes_g) * slots + (c % lanes_g) // 2, -1
    )
    expand = one_hot(iota((NCH, columns), 0), slot)
    chan8 = jnp.broadcast_to(chan_row[...].astype(jnp.float32), (8, NCH)).astype(jnp.bfloat16)
    chan_cols = dot(chan8, expand)[0:1, :]
    step = 128
    quarter = (iota((1, columns), 1) % 2).astype(jnp.float32) * 0.25
    for begin in range(0, FRAME, step):
        n = (iota((step, columns), 0) + begin).astype(jnp.float32)
        angle = n * chan_cols * (1.0 / FRAME) + quarter
        table[begin : begin + step, :] = cos_turns(angle, 1.0 / math.sqrt(FRAME)).astype(
            jnp.bfloat16
        )

    need = per_block * 2 * th
    span = need if need % 128 == 0 else chunk

    def merge_matrix(offset):
        k = iota((ng * span, BLOCK), 0)
        c = iota((ng * span, BLOCK), 1)
        return one_hot(k, ((c % total) // th) * span + (c // total) * th + c % th + offset)

    if span == need:
        merge[...] = merge_matrix(0)

    for load in loads[1:]:
        load.wait()
    b = beams
    eye = iota((b, b), 0) == iota((b, b), 1)
    spread = jnp.broadcast_to(pointing[...].astype(jnp.float32), (b, b))
    point_col = jnp.sum(jnp.where(eye, spread, 0.0), axis=1, keepdims=True).astype(jnp.int32)
    points = delays.shape[0]
    pick = one_hot(iota((b, points), 1), jnp.broadcast_to(point_col, (b, points)))
    hi, mid, low = pieces(delays[...])
    chosen = (dot(pick, hi) + dot(pick, mid)) + dot(pick, low)
    order = one_hot(
        iota((inputs, inputs), 0), jnp.broadcast_to(amap[...], (inputs, inputs))
    )
    hi, mid, low = pieces(chosen)
    chosen = (dot(hi, order) + dot(mid, order)) + dot(low, order)
    turns[...] = jnp.zeros_like(turns)
    turns[0:b, :] = chosen * (1.0 / NCH)

    @pl.when(grp == 0)
    def _():
        halo[...] = jnp.zeros_like(halo)

    @pl.when(grp > 0)
    def _():
        halo_copy.wait_recv()

    frames = [halo[:, i * FRAME : (i + 1) * FRAME].astype(jnp.float32) for i in range(keep)]
    frames += [volts[:, i * FRAME : (i + 1) * FRAME].astype(jnp.float32) for i in range(th)]
    filtered = []
    for t in range(th):
        value = pfb[0:1, :] * frames[t + keep]
        for tap in range(1, TAPS):
            value = value + pfb[tap : tap + 1, :] * frames[t + keep - tap]
        filtered.append(value.astype(jnp.bfloat16))
    filtered = jnp.concatenate(filtered, axis=0)
    made = dot(filtered, table[...]).astype(jnp.bfloat16)
    for g in range(ng):
        flat = jnp.concatenate(
            [
                made[t * here : (t + 1) * here, g * lanes_g : (g + 1) * lanes_g]
                for t in range(th)
            ],
            axis=1,
        )
        sent[g] = dot(flat, place[...]).astype(jnp.bfloat16)

    parts = blocks if span == need else 1

    def turn_copy(q, d):
        peer = grp_peer(d)
        lanes = pl.ds(q * span, span)
        return pltpu.make_async_remote_copy(
            src_ref=sent.at[peer, :, lanes],
            dst_ref=got.at[grp, :, lanes],
            send_sem=turn_send.at[q, d],
            recv_sem=turn_recv.at[q, d],
            device_id=(sect, peer),
            device_id_type=MESH,
        )

    for q in range(parts):
        for d in range(1, ng):
            turn_copy(q, d).start()

    mine = rows_of(sect)

    def begun(way, k):
        return lax.rem(row - way * k + 2 * outer, outer)

    def line_copy(way, q, k, block):
        at = rows_of(block * inner + col)
        return pltpu.make_async_remote_copy(
            src_ref=spec.at[q, at, :],
            dst_ref=spec.at[q, at, :],
            send_sem=line_send.at[(1 - way) // 2, q, k],
            recv_sem=line_recv.at[(1 - way) // 2, q, k],
            device_id=(lax.rem(row + way + outer, outer) * inner + col, grp),
            device_id_type=MESH,
        )

    def near_copy(q, d, mirrored):
        at = rows_of(begun(1, d) * inner + (1 - col if mirrored else col))
        return pltpu.make_async_remote_copy(
            src_ref=spec.at[q, at, :],
            dst_ref=spec.at[q, at, :],
            send_sem=near_send.at[q, d],
            recv_sem=near_recv.at[q, d],
            device_id=(row * inner + 1 - col, grp),
            device_id_type=MESH,
        )

    def extra_copy(way, q, block):
        at = rows_of(block * inner + 1 - col)
        return pltpu.make_async_remote_copy(
            src_ref=spec.at[q, at, :],
            dst_ref=spec.at[q, at, :],
            send_sem=extra_send.at[(1 - way) // 2, q],
            recv_sem=extra_recv.at[(1 - way) // 2, q],
            device_id=(lax.rem(row + way + outer, outer) * inner + col, grp),
            device_id_type=MESH,
        )

    def has_next(way):
        return row < outer - 1 if way == 1 else row > 0

    def has_behind(way, k):
        return row >= k if way == 1 else row + k < outer

    spare = [q for q in range(blocks) if q >= blocks // 2] if inner == 2 and outer > 3 else []

    def by_line(q, d):
        if q not in spare:
            return None
        if d == outer - 1:
            return row == 0
        if d == 1:
            return row == outer - 1
        return None

    def near_do(q, d, act):
        skip = by_line(q, d)
        if skip is None:
            act()
        else:
            pl.when(jnp.logical_not(skip))(act)

    for q in range(blocks):
        if q < parts:
            for d in range(1, ng):
                turn_copy(q, d).wait_recv()
        begin = q * need if span == need else 0
        flat = jnp.concatenate(
            [
                jnp.where(grp == g, sent[g, :, begin : begin + span], got[g, :, begin : begin + span])
                for g in range(ng)
            ],
            axis=1,
        )
        matrix = merge[...] if span == need else merge_matrix(q * need)
        spec[q, mine, :] = dot(flat, matrix).astype(jnp.bfloat16)
        for way in (1, -1):

            @pl.when(has_next(way))
            def _():
                line_copy(way, q, 0, row).start()

        if inner == 2:
            near_copy(q, 0, False).start()

    scale = 1.0 / math.sqrt(inputs)

    def weigh(tile):
        for k in range(per_tile):
            channel = chan[grp * slots + tile * per_tile + k].astype(jnp.float32) + 0.5
            for part in range(2):
                at = (k * 2 + part) * brows
                weights[tile, at : at + brows, :] = cos_turns(
                    turns[...] * channel + 0.25 * part, scale
                ).astype(jnp.bfloat16)

    steps = max(1, (outer - 1) * blocks)
    count = blocks * tiles
    for k in range(1, outer):
        for q in range(blocks):
            n = (k - 1) * blocks + q
            pl.loop(n * count // steps, (n + 1) * count // steps)(weigh)
            for way in (1, -1):

                @pl.when(has_behind(way, k))
                def _():
                    block = begun(way, k)
                    line_copy(way, q, k - 1, block).wait_recv()
                    if k < outer - 1:

                        @pl.when(has_next(way))
                        def _():
                            line_copy(way, q, k, block).start()

                    if inner == 2:
                        d = k if way == 1 else outer - k
                        near_do(q, d, lambda: near_copy(q, d, False).start())

    if outer == 1:
        pl.loop(0, count)(weigh)
    for way in (1, -1):
        last_but_one = row == (outer - 2 if way == 1 else 1)

        if spare:

            @pl.when(last_but_one)
            def _():
                for q in spare:
                    near_copy(q, 0, True).wait_recv()
                    extra_copy(way, q, row).start()

    lane = iota((brows, width), 1)
    slot_in = lane // (2 * total)
    first = (lane // total) % 2 == 0
    out_copies = []
    power[ng] = jnp.zeros_like(power[ng])
    acc = jnp.zeros((brows, width), jnp.float32)
    for q in range(blocks):
        if inner == 2:
            for d in range(outer):
                if not (d == 0 and q in spare):
                    near_do(q, d, lambda: near_copy(q, d, True).wait_recv())
        if q in spare:
            @pl.when((row != 1) & (row != outer - 2))
            def _():
                near_copy(q, 0, True).wait_recv()

            for way in (1, -1):

                @pl.when(row == (outer - 1 if way == 1 else 0))
                def _():
                    extra_copy(way, q, begun(way, 1)).wait_recv()

        copy = pltpu.make_async_copy(spec.at[q], gathered.at[q], out_sem.at[q])
        copy.start()
        out_copies.append(copy)
        for i in range(tiles):
            data = spec[q, :, i * width : (i + 1) * width]
            mixed = dot(weights[q * tiles + i], data)
            both = []
            for part in range(2):
                picked = jnp.zeros((brows, width), jnp.float32)
                for k in range(per_tile):
                    at = (k * 2 + part) * brows
                    picked = jnp.where(slot_in == k, mixed[at : at + brows, :], picked)
                both.append(picked)
            forward = pltpu.roll(both[1], total, 1)
            backward = pltpu.roll(both[1], width - total, 1)
            beam = both[0] + jnp.where(first, -backward, forward)
            acc = acc + beam * beam
    shift = width // 2
    while shift >= total:
        acc = acc + pltpu.roll(acc, shift, 1)
        shift //= 2
    power[ng] = acc[:, : power.shape[2]]

    beam_copies = []
    for d in range(1, ng):
        copy = pltpu.make_async_remote_copy(
            src_ref=power.at[ng],
            dst_ref=power.at[d],
            send_sem=beam_send.at[d],
            recv_sem=beam_recv.at[d],
            device_id=(sect, grp_peer(d)),
            device_id_type=MESH,
        )
        copy.start()
        beam_copies.append(copy)
    for q in range(blocks):
        for way in (1, -1):
            for k in range(outer - 1):

                @pl.when(has_behind(way, k) & has_next(way))
                def _():
                    line_copy(way, q, k, begun(way, k)).wait_send()

            if q in spare:

                @pl.when(row == (outer - 2 if way == 1 else 1))
                def _():
                    extra_copy(way, q, row).wait_send()

        if inner == 2:
            for d in range(outer):
                near_do(q, d, lambda: near_copy(q, d, False).wait_send())
    for q in range(parts):
        for d in range(1, ng):
            turn_copy(q, d).wait_send()

    @pl.when(grp < ng - 1)
    def _():
        halo_copy.wait_send()

    for copy in out_copies:
        copy.wait()
    summed = power[ng]
    for d, copy in enumerate(beam_copies):
        copy.wait_recv()
        summed = summed + power[d + 1]
    lanes = summed.shape[1]
    turned = pltpu.roll(summed, lax.rem(lanes - grp * th, lanes), 1)
    series[...] = turned[:beams, :th] * (1.0 / math.sqrt(NCH))
    for copy in beam_copies:
        copy.wait_send()


def vis_kernel(here, total, per_tile, tiles, spec, power, vis, series):
    width = spec.shape[2] // tiles
    series[...] = power[...]
    mine = pl.ds(pl.multiple_of(lax.axis_index("sect") * here, 16), here)
    lane = iota((here, width), 1)
    slot_in = lane // (2 * total)
    first = (lane // total) % 2 == 0
    for i in range(tiles):
        cols = slice(i * width, (i + 1) * width)
        local = spec[0, mine, cols].astype(jnp.float32)
        forward = pltpu.roll(local, total, 1)
        backward = pltpu.roll(local, width - total, 1)
        swapped = jnp.where(first, backward, -forward)
        left = []
        for k in range(per_tile):
            for part in (local, swapped):
                left.append(jnp.where(slot_in == k, part, 0.0).astype(jnp.bfloat16))
        block = dot(jnp.concatenate(left, axis=0), spec[0, :, cols], ((1,), (1,)))
        block = block * (1.0 / total)
        for k in range(per_tile):
            for part in range(2):
                at = (k * 2 + part) * here
                vis[i * per_tile + k, part] = block[at : at + here, :]


def per_device(ns, ng, volts, pfb_window, chan_order, delays, antenna_map, pointing):
    here = volts.shape[0]
    th = volts.shape[1] // FRAME
    inputs = delays.shape[1]
    beams = pointing.shape[0]
    slots = NCH // ng
    total = th * ng
    brows = round_up(beams, 16)
    lanes_g = round_up(2 * slots, 128)
    chunk = round_up(2 * slots * th, 128)
    blocks = NCH * 2 * th // BLOCK
    width = max(128, 2 * total)
    per_tile = width // (2 * total)
    tiles = BLOCK // width
    need = BLOCK // (2 * total) * 2 * th
    span = need if need % 128 == 0 else chunk
    outer = ns // 2 if ns % 2 == 0 else ns
    bf16, f32 = jnp.bfloat16, jnp.float32
    vmem = pl.BlockSpec(memory_space=pltpu.VMEM)
    hbm = pl.BlockSpec(memory_space=pltpu.HBM)
    parts = blocks if need % 128 == 0 else 1
    dims = (ns, ng, slots, here, th, inputs, beams)
    dma = pltpu.SemaphoreType.DMA
    gathered, series = pl.pallas_call(
        functools.partial(gather_kernel, dims),
        out_shape=(
            jax.ShapeDtypeStruct((blocks, inputs, BLOCK), bf16),
            jax.ShapeDtypeStruct((beams, th), f32),
        ),
        in_specs=[hbm, hbm, hbm, pl.BlockSpec(memory_space=pltpu.SMEM), hbm, hbm, hbm],
        out_specs=(pl.BlockSpec(memory_space=pl.ANY), vmem),
        scratch_shapes=[
            pltpu.VMEM(volts.shape, bf16),
            pltpu.VMEM(pfb_window.shape, f32),
            pltpu.VMEM((1, NCH), jnp.int32),
            pltpu.VMEM(delays.shape, f32),
            pltpu.VMEM((1, inputs), jnp.int32),
            pltpu.VMEM((1, beams), jnp.int32),
            dma((6,)),
            pltpu.VMEM((here, (TAPS - 1) * FRAME), bf16),
            pltpu.VMEM((FRAME, ng * lanes_g), bf16),
            pltpu.VMEM((th * lanes_g, chunk), bf16),
            pltpu.VMEM((ng * span, BLOCK), bf16),
            pltpu.VMEM((brows, inputs), f32),
            pltpu.VMEM((blocks * tiles, per_tile * 2 * brows, inputs), bf16),
            pltpu.VMEM((ng, here, chunk), bf16),
            pltpu.VMEM((ng, here, chunk), bf16),
            pltpu.VMEM((blocks, inputs, BLOCK), bf16),
            pltpu.VMEM((ng + 1, brows, round_up(total, 128)), f32),
            dma((2,)),
            dma((parts, ng)),
            dma((parts, ng)),
            dma((2, blocks, outer)),
            dma((2, blocks, outer)),
            dma((blocks, outer)),
            dma((blocks, outer)),
            dma((2, blocks)),
            dma((2, blocks)),
            dma((ng,)),
            dma((ng,)),
            dma((blocks,)),
        ],
        compiler_params=pltpu.CompilerParams(
            collective_id=0, has_side_effects=True, vmem_limit_bytes=48 * 1024 * 1024
        ),
    )(
        volts,
        pfb_window,
        chan_order,
        chan_order,
        delays,
        antenna_map,
        pointing,
    )
    split = 2 if tiles % 2 == 0 else 1
    small = pl.BlockSpec((beams, th), lambda q: (0, 0))
    vis, series = pl.pallas_call(
        functools.partial(vis_kernel, here, total, per_tile, tiles // split),
        grid=(blocks * split,),
        out_shape=(
            jax.ShapeDtypeStruct((slots, 2, here, inputs), f32),
            jax.ShapeDtypeStruct((beams, th), f32),
        ),
        in_specs=[
            pl.BlockSpec((1, inputs, BLOCK // split), lambda q: (q // split, 0, q % split)),
            small,
        ],
        out_specs=(
            pl.BlockSpec(
                (slots // (blocks * split), 2, here, inputs), lambda q: (q, 0, 0, 0)
            ),
            small,
        ),
        compiler_params=pltpu.CompilerParams(vmem_limit_bytes=48 * 1024 * 1024),
    )(gathered, series)
    return (vis, series)


def solution(mesh):
    ns, ng = mesh.shape["sect"], mesh.shape["grp"]
    return jax.shard_map(
        functools.partial(per_device, ns, ng),
        mesh=mesh,
        in_specs=(P("sect", "grp"), P(), P(), P(), P(), P("sect")),
        out_specs=(P("grp", None, "sect", None), P("sect", "grp")),
        check_vma=False,
    )
```

```python
import functools
import math

import jax
import jax.numpy as jnp
import numpy as np
from jax import lax
from jax.experimental import pallas as pl
from jax.experimental.pallas import tpu as pltpu
from jax.sharding import PartitionSpec as P

NCH = 256
TAPS = 4
FRAME = 2 * NCH
BLOCK = 512
MESH = pl.DeviceIdType.MESH


def round_up(n, m):
    return -(-n // m) * m


def cos_fit(degree):
    nodes = 0.125 + 0.125 * np.cos(np.pi * (np.arange(64) + 0.5) / 64)
    fit = np.polynomial.chebyshev.Chebyshev.fit(
        nodes, np.cos(2 * np.pi * np.sqrt(nodes)), degree, domain=[0.0, 0.25]
    )
    return [float(c) for c in fit.convert(kind=np.polynomial.Polynomial).coef]


COS = cos_fit(6)


def cos_turns(u, scale):
    r = u - jnp.round(u)
    y = r * r
    total = jnp.full_like(y, COS[-1] * scale)
    for c in COS[-2::-1]:
        total = total * y + c * scale
    return total


def dot(a, b, dims=((1,), (0,))):
    return lax.dot_general(a, b, (dims, ((), ())), preferred_element_type=jnp.float32)


def pieces(x):
    hi = x.astype(jnp.bfloat16)
    rest = x - hi.astype(jnp.float32)
    mid = rest.astype(jnp.bfloat16)
    low = (rest - mid.astype(jnp.float32)).astype(jnp.bfloat16)
    return hi, mid, low


def one_hot(rows, cols):
    return jnp.where(rows == cols, 1.0, 0.0).astype(jnp.bfloat16)


def iota(shape, dim):
    return lax.broadcasted_iota(jnp.int32, shape, dim)


def gather_kernel(
    dims,
    volts_in, pfb_in, chan_in, chan, delays_in, amap_in, pointing_in,
    gathered, series,
    volts, pfb, chan_row, delays, amap, pointing, in_sem,
    halo, table, place, merge, turns, weights, sent, got, spec, power,
    halo_sem, turn_send, turn_recv, line_send, line_recv, near_send, near_recv,
    extra_send, extra_recv, beam_send, beam_recv, out_sem,
):
    ns, ng, slots, here, th, inputs, beams = dims
    total = th * ng
    lanes_g = round_up(2 * slots, 128)
    chunk = sent.shape[2]
    blocks = NCH * 2 * th // BLOCK
    per_block = BLOCK // (2 * total)
    width = max(128, 2 * total)
    per_tile = width // (2 * total)
    tiles = BLOCK // width
    brows = turns.shape[0]
    inner = 2 if ns % 2 == 0 else 1
    outer = ns // inner

    sect = lax.axis_index("sect")
    grp = lax.axis_index("grp")
    row = sect // inner
    col = sect % inner

    def grp_peer(d):
        return lax.rem(grp + d, ng)

    barrier = pltpu.get_barrier_semaphore()
    for d in range(1, ng):
        pl.semaphore_signal(barrier, inc=1, device_id=(sect, grp_peer(d)), device_id_type=MESH)
    for way in (1, -1):

        @pl.when((row + way >= 0) & (row + way < outer))
        def _(way=way):
            pl.semaphore_signal(
                barrier, inc=1, device_id=((row + way) * inner + col, grp), device_id_type=MESH
            )

    if inner == 2:
        pl.semaphore_signal(
            barrier, inc=1, device_id=(row * inner + 1 - col, grp), device_id_type=MESH
        )

    loads = []
    operands = ((chan_in, chan_row.at[0]), (volts_in, volts), (pfb_in, pfb),
                (delays_in, delays), (amap_in, amap.at[0]), (pointing_in, pointing.at[0]))
    for at, (src, dst) in enumerate(operands):
        loads.append(pltpu.make_async_copy(src, dst, in_sem.at[at]))
        loads[-1].start()

    def rows_of(s):
        return pl.ds(pl.multiple_of(s * here, 16), here)

    k = iota((th * lanes_g, chunk), 0)
    c = iota((th * lanes_g, chunk), 1)
    place[...] = one_hot(k, (c % th) * lanes_g + c // th)

    in_line = (row > 0).astype(jnp.int32) + (row < outer - 1).astype(jnp.int32)
    pl.semaphore_wait(barrier, (ng - 1) + (inner - 1) + in_line)

    keep = TAPS - 1
    halo_copy = pltpu.make_async_remote_copy(
        src_ref=volts_in.at[:, (th - keep) * FRAME :],
        dst_ref=halo,
        send_sem=halo_sem.at[0],
        recv_sem=halo_sem.at[1],
        device_id=(sect, lax.rem(grp + 1, ng)),
        device_id_type=MESH,
    )

    @pl.when(grp < ng - 1)
    def _():
        halo_copy.start()

    loads[0].wait()
    columns = ng * lanes_g
    c = iota((NCH, columns), 1)
    slot = jnp.where(
        c % lanes_g < 2 * slots, (c // lanes_g) * slots + (c % lanes_g) // 2, -1
    )
    expand = one_hot(iota((NCH, columns), 0), slot)
    chan8 = jnp.broadcast_to(chan_row[...].astype(jnp.float32), (8, NCH)).astype(jnp.bfloat16)
    chan_cols = dot(chan8, expand)[0:1, :]
    step = 128
    quarter = (iota((1, columns), 1) % 2).astype(jnp.float32) * 0.25
    for begin in range(0, FRAME, step):
        n = (iota((step, columns), 0) + begin).astype(jnp.float32)
        angle = n * chan_cols * (1.0 / FRAME) + quarter
        table[begin : begin + step, :] = cos_turns(angle, 1.0 / math.sqrt(FRAME)).astype(
            jnp.bfloat16
        )

    need = per_block * 2 * th
    span = need if need % 128 == 0 else chunk

    def merge_matrix(offset):
        k = iota((ng * span, BLOCK), 0)
        c = iota((ng * span, BLOCK), 1)
        return one_hot(k, ((c % total) // th) * span + (c // total) * th + c % th + offset)

    if span == need:
        merge[...] = merge_matrix(0)

    for load in loads[1:]:
        load.wait()
    b = beams
    eye = iota((b, b), 0) == iota((b, b), 1)
    spread = jnp.broadcast_to(pointing[...].astype(jnp.float32), (b, b))
    point_col = jnp.sum(jnp.where(eye, spread, 0.0), axis=1, keepdims=True).astype(jnp.int32)
    points = delays.shape[0]
    pick = one_hot(iota((b, points), 1), jnp.broadcast_to(point_col, (b, points)))
    hi, mid, low = pieces(delays[...])
    chosen = (dot(pick, hi) + dot(pick, mid)) + dot(pick, low)
    order = one_hot(
        iota((inputs, inputs), 0), jnp.broadcast_to(amap[...], (inputs, inputs))
    )
    hi, mid, low = pieces(chosen)
    chosen = (dot(hi, order) + dot(mid, order)) + dot(low, order)
    turns[...] = jnp.zeros_like(turns)
    turns[0:b, :] = chosen * (1.0 / NCH)

    @pl.when(grp == 0)
    def _():
        halo[...] = jnp.zeros_like(halo)

    @pl.when(grp > 0)
    def _():
        halo_copy.wait_recv()

    frames = [halo[:, i * FRAME : (i + 1) * FRAME].astype(jnp.float32) for i in range(keep)]
    frames += [volts[:, i * FRAME : (i + 1) * FRAME].astype(jnp.float32) for i in range(th)]
    filtered = []
    for t in range(th):
        value = pfb[0:1, :] * frames[t + keep]
        for tap in range(1, TAPS):
            value = value + pfb[tap : tap + 1, :] * frames[t + keep - tap]
        filtered.append(value.astype(jnp.bfloat16))
    filtered = jnp.concatenate(filtered, axis=0)
    made = dot(filtered, table[...]).astype(jnp.bfloat16)
    for g in range(ng):
        flat = jnp.concatenate(
            [
                made[t * here : (t + 1) * here, g * lanes_g : (g + 1) * lanes_g]
                for t in range(th)
            ],
            axis=1,
        )
        sent[g] = dot(flat, place[...]).astype(jnp.bfloat16)

    parts = blocks if span == need else 1

    def turn_copy(q, d):
        peer = grp_peer(d)
        lanes = pl.ds(q * span, span)
        return pltpu.make_async_remote_copy(
            src_ref=sent.at[peer, :, lanes],
            dst_ref=got.at[grp, :, lanes],
            send_sem=turn_send.at[q, d],
            recv_sem=turn_recv.at[q, d],
            device_id=(sect, peer),
            device_id_type=MESH,
        )

    for q in range(parts):
        for d in range(1, ng):
            turn_copy(q, d).start()

    mine = rows_of(sect)

    def begun(way, k):
        return lax.rem(row - way * k + 2 * outer, outer)

    def line_copy(way, q, k, block):
        at = rows_of(block * inner + col)
        return pltpu.make_async_remote_copy(
            src_ref=spec.at[q, at, :],
            dst_ref=spec.at[q, at, :],
            send_sem=line_send.at[(1 - way) // 2, q, k],
            recv_sem=line_recv.at[(1 - way) // 2, q, k],
            device_id=(lax.rem(row + way + outer, outer) * inner + col, grp),
            device_id_type=MESH,
        )

    def near_copy(q, d, mirrored):
        at = rows_of(begun(1, d) * inner + (1 - col if mirrored else col))
        return pltpu.make_async_remote_copy(
            src_ref=spec.at[q, at, :],
            dst_ref=spec.at[q, at, :],
            send_sem=near_send.at[q, d],
            recv_sem=near_recv.at[q, d],
            device_id=(row * inner + 1 - col, grp),
            device_id_type=MESH,
        )

    def extra_copy(way, q, block):
        at = rows_of(block * inner + 1 - col)
        return pltpu.make_async_remote_copy(
            src_ref=spec.at[q, at, :],
            dst_ref=spec.at[q, at, :],
            send_sem=extra_send.at[(1 - way) // 2, q],
            recv_sem=extra_recv.at[(1 - way) // 2, q],
            device_id=(lax.rem(row + way + outer, outer) * inner + col, grp),
            device_id_type=MESH,
        )

    def has_next(way):
        return row < outer - 1 if way == 1 else row > 0

    def has_behind(way, k):
        return row >= k if way == 1 else row + k < outer

    spare = [q for q in range(blocks) if q >= blocks // 2] if inner == 2 and outer > 3 else []

    def passes_on(way):
        if way == 1:
            return (row == 0) | (row == outer - 2)
        return (row == 1) | (row == outer - 1)

    def pass_on(at_end):
        for way in (1, -1):
            end = row == (0 if way == 1 else outer - 1)
            last = row == (outer - 2 if way == 1 else 1)

            @pl.when(end if at_end else last)
            def _():
                for q in spare:
                    near_copy(q, 0, True).wait_recv()
                    extra_copy(way, q, row).start()

    def by_line(q, d):
        if q not in spare:
            return None
        if d == outer - 1:
            return passes_on(1)
        if d == 1:
            return passes_on(-1)
        return None

    def near_do(q, d, act):
        skip = by_line(q, d)
        if skip is None:
            act()
        else:
            pl.when(jnp.logical_not(skip))(act)

    for q in range(blocks):
        if q < parts:
            for d in range(1, ng):
                turn_copy(q, d).wait_recv()
        begin = q * need if span == need else 0
        flat = jnp.concatenate(
            [
                jnp.where(grp == g, sent[g, :, begin : begin + span], got[g, :, begin : begin + span])
                for g in range(ng)
            ],
            axis=1,
        )
        matrix = merge[...] if span == need else merge_matrix(q * need)
        spec[q, mine, :] = dot(flat, matrix).astype(jnp.bfloat16)
        for way in (1, -1):

            @pl.when(has_next(way))
            def _():
                line_copy(way, q, 0, row).start()

        if inner == 2:
            near_copy(q, 0, False).start()

    scale = 1.0 / math.sqrt(inputs)

    def weigh(tile):
        for k in range(per_tile):
            channel = chan[grp * slots + tile * per_tile + k].astype(jnp.float32) + 0.5
            for part in range(2):
                at = (k * 2 + part) * brows
                weights[tile, at : at + brows, :] = cos_turns(
                    turns[...] * channel + 0.25 * part, scale
                ).astype(jnp.bfloat16)

    steps = max(1, (outer - 1) * blocks)
    count = blocks * tiles
    for k in range(1, outer):
        for q in range(blocks):
            n = (k - 1) * blocks + q
            pl.loop(n * count // steps, (n + 1) * count // steps)(weigh)
            for way in (1, -1):

                @pl.when(has_behind(way, k))
                def _():
                    block = begun(way, k)
                    line_copy(way, q, k - 1, block).wait_recv()
                    if k < outer - 1:

                        @pl.when(has_next(way))
                        def _():
                            line_copy(way, q, k, block).start()

                    if inner == 2:
                        d = k if way == 1 else outer - k
                        near_do(q, d, lambda: near_copy(q, d, False).start())

        if k == 1 and spare:
            pass_on(True)

    if outer == 1:
        pl.loop(0, count)(weigh)
    if spare:
        pass_on(False)

    lane = iota((brows, width), 1)
    slot_in = lane // (2 * total)
    first = (lane // total) % 2 == 0
    out_copies = []
    power[ng] = jnp.zeros_like(power[ng])
    acc = jnp.zeros((brows, width), jnp.float32)
    for q in range(blocks):
        if inner == 2:
            for d in range(outer):
                if not (d == 0 and q in spare):
                    near_do(q, d, lambda: near_copy(q, d, True).wait_recv())
        if q in spare:
            @pl.when(jnp.logical_not(passes_on(1) | passes_on(-1)))
            def _():
                near_copy(q, 0, True).wait_recv()

            for way in (1, -1):

                @pl.when(passes_on(-way))
                def _():
                    extra_copy(way, q, begun(way, 1)).wait_recv()

        copy = pltpu.make_async_copy(spec.at[q], gathered.at[q], out_sem.at[q])
        copy.start()
        out_copies.append(copy)
        for i in range(tiles):
            data = spec[q, :, i * width : (i + 1) * width]
            mixed = dot(weights[q * tiles + i], data)
            both = []
            for part in range(2):
                picked = jnp.zeros((brows, width), jnp.float32)
                for k in range(per_tile):
                    at = (k * 2 + part) * brows
                    picked = jnp.where(slot_in == k, mixed[at : at + brows, :], picked)
                both.append(picked)
            forward = pltpu.roll(both[1], total, 1)
            backward = pltpu.roll(both[1], width - total, 1)
            beam = both[0] + jnp.where(first, -backward, forward)
            acc = acc + beam * beam
    shift = width // 2
    while shift >= total:
        acc = acc + pltpu.roll(acc, shift, 1)
        shift //= 2
    power[ng] = acc[:, : power.shape[2]]

    beam_copies = []
    for d in range(1, ng):
        copy = pltpu.make_async_remote_copy(
            src_ref=power.at[ng],
            dst_ref=power.at[d],
            send_sem=beam_send.at[d],
            recv_sem=beam_recv.at[d],
            device_id=(sect, grp_peer(d)),
            device_id_type=MESH,
        )
        copy.start()
        beam_copies.append(copy)
    for q in range(blocks):
        for way in (1, -1):
            for k in range(outer - 1):

                @pl.when(has_behind(way, k) & has_next(way))
                def _():
                    line_copy(way, q, k, begun(way, k)).wait_send()

            if q in spare:

                @pl.when(passes_on(way))
                def _():
                    extra_copy(way, q, row).wait_send()

        if inner == 2:
            for d in range(outer):
                near_do(q, d, lambda: near_copy(q, d, False).wait_send())
    for q in range(parts):
        for d in range(1, ng):
            turn_copy(q, d).wait_send()

    @pl.when(grp < ng - 1)
    def _():
        halo_copy.wait_send()

    for copy in out_copies:
        copy.wait()
    summed = power[ng]
    for d, copy in enumerate(beam_copies):
        copy.wait_recv()
        summed = summed + power[d + 1]
    lanes = summed.shape[1]
    turned = pltpu.roll(summed, lax.rem(lanes - grp * th, lanes), 1)
    series[...] = turned.T[:th, :beams] * (1.0 / math.sqrt(NCH))
    for copy in beam_copies:
        copy.wait_send()


def vis_kernel(here, total, per_tile, tiles, spec, vis):
    width = spec.shape[2] // tiles
    mine = pl.ds(pl.multiple_of(lax.axis_index("sect") * here, 16), here)
    lane = iota((here, width), 1)
    slot_in = lane // (2 * total)
    first = (lane // total) % 2 == 0
    for i in range(tiles):
        cols = slice(i * width, (i + 1) * width)
        local = spec[0, mine, cols].astype(jnp.float32)
        forward = pltpu.roll(local, total, 1)
        backward = pltpu.roll(local, width - total, 1)
        swapped = jnp.where(first, backward, -forward)
        left = []
        for k in range(per_tile):
            for part in (local, swapped):
                left.append(jnp.where(slot_in == k, part, 0.0).astype(jnp.bfloat16))
        block = dot(jnp.concatenate(left, axis=0), spec[0, :, cols], ((1,), (1,)))
        block = block * (1.0 / total)
        for k in range(per_tile):
            for part in range(2):
                at = (k * 2 + part) * here
                vis[i * per_tile + k, part] = block[at : at + here, :]


def per_device(ns, ng, volts, pfb_window, chan_order, delays, antenna_map, pointing):
    here = volts.shape[0]
    th = volts.shape[1] // FRAME
    inputs = delays.shape[1]
    beams = pointing.shape[0]
    slots = NCH // ng
    total = th * ng
    brows = round_up(beams, 16)
    lanes_g = round_up(2 * slots, 128)
    chunk = round_up(2 * slots * th, 128)
    blocks = NCH * 2 * th // BLOCK
    width = max(128, 2 * total)
    per_tile = width // (2 * total)
    tiles = BLOCK // width
    need = BLOCK // (2 * total) * 2 * th
    span = need if need % 128 == 0 else chunk
    outer = ns // 2 if ns % 2 == 0 else ns
    bf16, f32 = jnp.bfloat16, jnp.float32
    vmem = pl.BlockSpec(memory_space=pltpu.VMEM)
    hbm = pl.BlockSpec(memory_space=pltpu.HBM)
    parts = blocks if need % 128 == 0 else 1
    dims = (ns, ng, slots, here, th, inputs, beams)
    dma = pltpu.SemaphoreType.DMA
    gathered, series = pl.pallas_call(
        functools.partial(gather_kernel, dims),
        out_shape=(
            jax.ShapeDtypeStruct((blocks, inputs, BLOCK), bf16),
            jax.ShapeDtypeStruct((th, beams), f32),
        ),
        in_specs=[hbm, hbm, hbm, pl.BlockSpec(memory_space=pltpu.SMEM), hbm, hbm, hbm],
        out_specs=(pl.BlockSpec(memory_space=pl.ANY), vmem),
        scratch_shapes=[
            pltpu.VMEM(volts.shape, bf16),
            pltpu.VMEM(pfb_window.shape, f32),
            pltpu.VMEM((1, NCH), jnp.int32),
            pltpu.VMEM(delays.shape, f32),
            pltpu.VMEM((1, inputs), jnp.int32),
            pltpu.VMEM((1, beams), jnp.int32),
            dma((6,)),
            pltpu.VMEM((here, (TAPS - 1) * FRAME), bf16),
            pltpu.VMEM((FRAME, ng * lanes_g), bf16),
            pltpu.VMEM((th * lanes_g, chunk), bf16),
            pltpu.VMEM((ng * span, BLOCK), bf16),
            pltpu.VMEM((brows, inputs), f32),
            pltpu.VMEM((blocks * tiles, per_tile * 2 * brows, inputs), bf16),
            pltpu.VMEM((ng, here, chunk), bf16),
            pltpu.VMEM((ng, here, chunk), bf16),
            pltpu.VMEM((blocks, inputs, BLOCK), bf16),
            pltpu.VMEM((ng + 1, brows, round_up(total, 128)), f32),
            dma((2,)),
            dma((parts, ng)),
            dma((parts, ng)),
            dma((2, blocks, outer)),
            dma((2, blocks, outer)),
            dma((blocks, outer)),
            dma((blocks, outer)),
            dma((2, blocks)),
            dma((2, blocks)),
            dma((ng,)),
            dma((ng,)),
            dma((blocks,)),
        ],
        compiler_params=pltpu.CompilerParams(
            collective_id=0, has_side_effects=True, vmem_limit_bytes=63 * 1024 * 1024
        ),
    )(
        volts,
        pfb_window,
        chan_order,
        chan_order,
        delays,
        antenna_map,
        pointing,
    )
    vis = pl.pallas_call(
        functools.partial(vis_kernel, here, total, per_tile, tiles),
        grid=(blocks,),
        out_shape=jax.ShapeDtypeStruct((slots, 2, here, inputs), f32),
        in_specs=[pl.BlockSpec((1, inputs, BLOCK), lambda q: (q, 0, 0))],
        out_specs=pl.BlockSpec(
            (slots // blocks, 2, here, inputs), lambda q: (q, 0, 0, 0)
        ),
        compiler_params=pltpu.CompilerParams(vmem_limit_bytes=63 * 1024 * 1024),
    )(gathered)
    return (vis, series.T)


def solution(mesh):
    ns, ng = mesh.shape["sect"], mesh.shape["grp"]
    return jax.shard_map(
        functools.partial(per_device, ns, ng),
        mesh=mesh,
        in_specs=(P("sect", "grp"), P(), P(), P(), P(), P("sect")),
        out_specs=(P("grp", None, "sect", None), P("sect", "grp")),
        check_vma=False,
    )
```

```python
import functools
import math

import jax
import jax.numpy as jnp
import numpy as np
from jax import lax
from jax.experimental import pallas as pl
from jax.experimental.pallas import tpu as pltpu
from jax.sharding import PartitionSpec as P

NCH = 256
TAPS = 4
FRAME = 2 * NCH
BLOCK = 512
MESH = pl.DeviceIdType.MESH


def round_up(n, m):
    return -(-n // m) * m


def cos_fit(degree):
    nodes = 0.125 + 0.125 * np.cos(np.pi * (np.arange(64) + 0.5) / 64)
    fit = np.polynomial.chebyshev.Chebyshev.fit(
        nodes, np.cos(2 * np.pi * np.sqrt(nodes)), degree, domain=[0.0, 0.25]
    )
    return [float(c) for c in fit.convert(kind=np.polynomial.Polynomial).coef]


COS = cos_fit(6)


def cos_turns(u, scale):
    r = u - jnp.round(u)
    y = r * r
    total = jnp.full_like(y, COS[-1] * scale)
    for c in COS[-2::-1]:
        total = total * y + c * scale
    return total


def dot(a, b, dims=((1,), (0,))):
    return lax.dot_general(a, b, (dims, ((), ())), preferred_element_type=jnp.float32)


def pieces(x):
    hi = x.astype(jnp.bfloat16)
    rest = x - hi.astype(jnp.float32)
    mid = rest.astype(jnp.bfloat16)
    low = (rest - mid.astype(jnp.float32)).astype(jnp.bfloat16)
    return hi, mid, low


def one_hot(rows, cols):
    return jnp.where(rows == cols, 1.0, 0.0).astype(jnp.bfloat16)


def iota(shape, dim):
    return lax.broadcasted_iota(jnp.int32, shape, dim)


def gather_kernel(
    dims,
    volts_in, pfb_in, chan_in, chan, delays_in, amap_in, pointing_in,
    gathered, series,
    volts, pfb, chan_row, delays, amap, pointing, in_sem,
    halo, table, place, merge, turns, weights, sent, got, spec, power,
    halo_sem, turn_send, turn_recv, line_send, line_recv, near_send, near_recv,
    extra_send, extra_recv, beam_send, beam_recv, out_sem,
):
    ns, ng, slots, here, th, inputs, beams = dims
    total = th * ng
    lanes_g = round_up(2 * slots, 128)
    chunk = sent.shape[2]
    blocks = NCH * 2 * th // BLOCK
    per_block = BLOCK // (2 * total)
    width = max(128, 2 * total)
    per_tile = width // (2 * total)
    tiles = BLOCK // width
    brows = turns.shape[0]
    inner = 2 if ns % 2 == 0 else 1
    outer = ns // inner

    sect = lax.axis_index("sect")
    grp = lax.axis_index("grp")
    row = sect // inner
    col = sect % inner

    def grp_peer(d):
        return lax.rem(grp + d, ng)

    barrier = pltpu.get_barrier_semaphore()
    for d in range(1, ng):
        pl.semaphore_signal(barrier, inc=1, device_id=(sect, grp_peer(d)), device_id_type=MESH)
    for way in (1, -1):

        @pl.when((row + way >= 0) & (row + way < outer))
        def _(way=way):
            pl.semaphore_signal(
                barrier, inc=1, device_id=((row + way) * inner + col, grp), device_id_type=MESH
            )

    if inner == 2:
        pl.semaphore_signal(
            barrier, inc=1, device_id=(row * inner + 1 - col, grp), device_id_type=MESH
        )

    loads = []
    operands = ((chan_in, chan_row.at[0]), (volts_in, volts), (pfb_in, pfb),
                (delays_in, delays), (amap_in, amap.at[0]), (pointing_in, pointing.at[0]))
    for at, (src, dst) in enumerate(operands):
        loads.append(pltpu.make_async_copy(src, dst, in_sem.at[at]))
        loads[-1].start()

    def rows_of(s):
        return pl.ds(pl.multiple_of(s * here, 16), here)

    k = iota((th * lanes_g, chunk), 0)
    c = iota((th * lanes_g, chunk), 1)
    place[...] = one_hot(k, (c % th) * lanes_g + c // th)

    in_line = (row > 0).astype(jnp.int32) + (row < outer - 1).astype(jnp.int32)
    pl.semaphore_wait(barrier, (ng - 1) + (inner - 1) + in_line)

    keep = TAPS - 1
    halo_copy = pltpu.make_async_remote_copy(
        src_ref=volts_in.at[:, (th - keep) * FRAME :],
        dst_ref=halo,
        send_sem=halo_sem.at[0],
        recv_sem=halo_sem.at[1],
        device_id=(sect, lax.rem(grp + 1, ng)),
        device_id_type=MESH,
    )

    @pl.when(grp < ng - 1)
    def _():
        halo_copy.start()

    loads[0].wait()
    columns = ng * lanes_g
    c = iota((NCH, columns), 1)
    slot = jnp.where(
        c % lanes_g < 2 * slots, (c // lanes_g) * slots + (c % lanes_g) // 2, -1
    )
    expand = one_hot(iota((NCH, columns), 0), slot)
    chan8 = jnp.broadcast_to(chan_row[...].astype(jnp.float32), (8, NCH)).astype(jnp.bfloat16)
    chan_cols = dot(chan8, expand)[0:1, :]
    step = 128
    quarter = (iota((1, columns), 1) % 2).astype(jnp.float32) * 0.25
    for begin in range(0, FRAME, step):
        n = (iota((step, columns), 0) + begin).astype(jnp.float32)
        angle = n * chan_cols * (1.0 / FRAME) + quarter
        table[begin : begin + step, :] = cos_turns(angle, 1.0 / math.sqrt(FRAME)).astype(
            jnp.bfloat16
        )

    need = per_block * 2 * th
    span = need if need % 128 == 0 else chunk

    def merge_matrix(offset):
        k = iota((ng * span, BLOCK), 0)
        c = iota((ng * span, BLOCK), 1)
        return one_hot(k, ((c % total) // th) * span + (c // total) * th + c % th + offset)

    if span == need:
        merge[...] = merge_matrix(0)

    for load in loads[1:]:
        load.wait()
    b = beams
    eye = iota((b, b), 0) == iota((b, b), 1)
    spread = jnp.broadcast_to(pointing[...].astype(jnp.float32), (b, b))
    point_col = jnp.sum(jnp.where(eye, spread, 0.0), axis=1, keepdims=True).astype(jnp.int32)
    points = delays.shape[0]
    pick = one_hot(iota((b, points), 1), jnp.broadcast_to(point_col, (b, points)))
    hi, mid, low = pieces(delays[...])
    chosen = (dot(pick, hi) + dot(pick, mid)) + dot(pick, low)
    order = one_hot(
        iota((inputs, inputs), 0), jnp.broadcast_to(amap[...], (inputs, inputs))
    )
    hi, mid, low = pieces(chosen)
    chosen = (dot(hi, order) + dot(mid, order)) + dot(low, order)
    turns[...] = jnp.zeros_like(turns)
    turns[0:b, :] = chosen * (1.0 / NCH)

    @pl.when(grp == 0)
    def _():
        halo[...] = jnp.zeros_like(halo)

    @pl.when(grp > 0)
    def _():
        halo_copy.wait_recv()

    frames = [halo[:, i * FRAME : (i + 1) * FRAME].astype(jnp.float32) for i in range(keep)]
    frames += [volts[:, i * FRAME : (i + 1) * FRAME].astype(jnp.float32) for i in range(th)]
    filtered = []
    for t in range(th):
        value = pfb[0:1, :] * frames[t + keep]
        for tap in range(1, TAPS):
            value = value + pfb[tap : tap + 1, :] * frames[t + keep - tap]
        filtered.append(value.astype(jnp.bfloat16))
    filtered = jnp.concatenate(filtered, axis=0)
    made = dot(filtered, table[...]).astype(jnp.bfloat16)
    for g in range(ng):
        flat = jnp.concatenate(
            [
                made[t * here : (t + 1) * here, g * lanes_g : (g + 1) * lanes_g]
                for t in range(th)
            ],
            axis=1,
        )
        sent[g] = dot(flat, place[...]).astype(jnp.bfloat16)

    parts = blocks if span == need else 1

    def turn_copy(q, d):
        peer = grp_peer(d)
        lanes = pl.ds(q * span, span)
        return pltpu.make_async_remote_copy(
            src_ref=sent.at[peer, :, lanes],
            dst_ref=got.at[grp, :, lanes],
            send_sem=turn_send.at[q, d],
            recv_sem=turn_recv.at[q, d],
            device_id=(sect, peer),
            device_id_type=MESH,
        )

    for q in range(parts):
        for d in range(1, ng):
            turn_copy(q, d).start()

    mine = rows_of(sect)

    def begun(way, k):
        return lax.rem(row - way * k + 2 * outer, outer)

    def line_copy(way, q, k, block):
        at = rows_of(block * inner + col)
        return pltpu.make_async_remote_copy(
            src_ref=spec.at[q, at, :],
            dst_ref=spec.at[q, at, :],
            send_sem=line_send.at[(1 - way) // 2, q, k],
            recv_sem=line_recv.at[(1 - way) // 2, q, k],
            device_id=(lax.rem(row + way + outer, outer) * inner + col, grp),
            device_id_type=MESH,
        )

    def near_copy(q, d, mirrored):
        at = rows_of(begun(1, d) * inner + (1 - col if mirrored else col))
        return pltpu.make_async_remote_copy(
            src_ref=spec.at[q, at, :],
            dst_ref=spec.at[q, at, :],
            send_sem=near_send.at[q, d],
            recv_sem=near_recv.at[q, d],
            device_id=(row * inner + 1 - col, grp),
            device_id_type=MESH,
        )

    def extra_copy(way, q, block):
        at = rows_of(block * inner + 1 - col)
        return pltpu.make_async_remote_copy(
            src_ref=spec.at[q, at, :],
            dst_ref=spec.at[q, at, :],
            send_sem=extra_send.at[(1 - way) // 2, q],
            recv_sem=extra_recv.at[(1 - way) // 2, q],
            device_id=(lax.rem(row + way + outer, outer) * inner + col, grp),
            device_id_type=MESH,
        )

    def has_next(way):
        return row < outer - 1 if way == 1 else row > 0

    def has_behind(way, k):
        return row >= k if way == 1 else row + k < outer

    spare = [q for q in range(blocks) if q >= blocks // 2] if inner == 2 and outer > 3 else []

    def passes_on(way):
        if way == 1:
            return (row == 0) | (row == outer - 2)
        return (row == 1) | (row == outer - 1)

    def pass_on(at_end):
        for way in (1, -1):
            end = row == (0 if way == 1 else outer - 1)
            last = row == (outer - 2 if way == 1 else 1)

            @pl.when(end if at_end else last)
            def _():
                for q in spare:
                    near_copy(q, 0, True).wait_recv()
                    extra_copy(way, q, row).start()

    def by_line(q, d):
        if q not in spare:
            return None
        if d == outer - 1:
            return passes_on(1)
        if d == 1:
            return passes_on(-1)
        return None

    def near_do(q, d, act):
        skip = by_line(q, d)
        if skip is None:
            act()
        else:
            pl.when(jnp.logical_not(skip))(act)

    for q in range(blocks):
        if q < parts:
            for d in range(1, ng):
                turn_copy(q, d).wait_recv()
        begin = q * need if span == need else 0
        flat = jnp.concatenate(
            [
                jnp.where(grp == g, sent[g, :, begin : begin + span], got[g, :, begin : begin + span])
                for g in range(ng)
            ],
            axis=1,
        )
        matrix = merge[...] if span == need else merge_matrix(q * need)
        spec[q, mine, :] = dot(flat, matrix).astype(jnp.bfloat16)
        for way in (1, -1):

            @pl.when(has_next(way))
            def _():
                line_copy(way, q, 0, row).start()

        if inner == 2:
            near_copy(q, 0, False).start()

    scale = 1.0 / math.sqrt(inputs)

    def weigh(tile):
        for k in range(per_tile):
            channel = chan[grp * slots + tile * per_tile + k].astype(jnp.float32) + 0.5
            for part in range(2):
                at = (k * 2 + part) * brows
                weights[tile, at : at + brows, :] = cos_turns(
                    turns[...] * channel + 0.25 * part, scale
                ).astype(jnp.bfloat16)

    steps = max(1, (outer - 1) * blocks)
    count = blocks * tiles
    for k in range(1, outer):
        for q in range(blocks):
            n = (k - 1) * blocks + q
            pl.loop(n * count // steps, (n + 1) * count // steps)(weigh)
            for way in (1, -1):

                @pl.when(has_behind(way, k))
                def _():
                    block = begun(way, k)
                    line_copy(way, q, k - 1, block).wait_recv()
                    if k < outer - 1:

                        @pl.when(has_next(way))
                        def _():
                            line_copy(way, q, k, block).start()

                    if inner == 2:
                        d = k if way == 1 else outer - k
                        near_do(q, d, lambda: near_copy(q, d, False).start())

        if k == 1 and spare:
            pass_on(True)

    if outer == 1:
        pl.loop(0, count)(weigh)
    if spare:
        pass_on(False)

    lane = iota((brows, width), 1)
    slot_in = lane // (2 * total)
    first = (lane // total) % 2 == 0
    out_copies = []
    power[ng] = jnp.zeros_like(power[ng])
    acc = jnp.zeros((brows, width), jnp.float32)
    for q in range(blocks):
        if inner == 2:
            for d in range(outer):
                if not (d == 0 and q in spare):
                    near_do(q, d, lambda: near_copy(q, d, True).wait_recv())
        if q in spare:
            @pl.when(jnp.logical_not(passes_on(1) | passes_on(-1)))
            def _():
                near_copy(q, 0, True).wait_recv()

            for way in (1, -1):

                @pl.when(passes_on(-way))
                def _():
                    extra_copy(way, q, begun(way, 1)).wait_recv()

        copy = pltpu.make_async_copy(spec.at[q], gathered.at[q], out_sem.at[q])
        copy.start()
        out_copies.append(copy)
        for i in range(tiles):
            data = spec[q, :, i * width : (i + 1) * width]
            mixed = dot(weights[q * tiles + i], data)
            both = []
            for part in range(2):
                picked = jnp.zeros((brows, width), jnp.float32)
                for k in range(per_tile):
                    at = (k * 2 + part) * brows
                    picked = jnp.where(slot_in == k, mixed[at : at + brows, :], picked)
                both.append(picked)
            forward = pltpu.roll(both[1], total, 1)
            backward = pltpu.roll(both[1], width - total, 1)
            beam = both[0] + jnp.where(first, -backward, forward)
            acc = acc + beam * beam
    shift = width // 2
    while shift >= total:
        acc = acc + pltpu.roll(acc, shift, 1)
        shift //= 2
    power[ng] = acc[:, : power.shape[2]]

    beam_copies = []
    for d in range(1, ng):
        copy = pltpu.make_async_remote_copy(
            src_ref=power.at[ng],
            dst_ref=power.at[d],
            send_sem=beam_send.at[d],
            recv_sem=beam_recv.at[d],
            device_id=(sect, grp_peer(d)),
            device_id_type=MESH,
        )
        copy.start()
        beam_copies.append(copy)
    for q in range(blocks):
        for way in (1, -1):
            for k in range(outer - 1):

                @pl.when(has_behind(way, k) & has_next(way))
                def _():
                    line_copy(way, q, k, begun(way, k)).wait_send()

            if q in spare:

                @pl.when(passes_on(way))
                def _():
                    extra_copy(way, q, row).wait_send()

        if inner == 2:
            for d in range(outer):
                near_do(q, d, lambda: near_copy(q, d, False).wait_send())
    for q in range(parts):
        for d in range(1, ng):
            turn_copy(q, d).wait_send()

    @pl.when(grp < ng - 1)
    def _():
        halo_copy.wait_send()

    for copy in out_copies:
        copy.wait()
    summed = power[ng]
    for d, copy in enumerate(beam_copies):
        copy.wait_recv()
        summed = summed + power[d + 1]
    lanes = summed.shape[1]
    turned = pltpu.roll(summed, lax.rem(lanes - grp * th, lanes), 1)
    series[...] = turned.T[:th, :beams] * (1.0 / math.sqrt(NCH))
    for copy in beam_copies:
        copy.wait_send()


def vis_kernel(here, total, per_tile, tiles, spec, vis):
    width = spec.shape[2] // tiles
    mine = pl.ds(pl.multiple_of(lax.axis_index("sect") * here, 16), here)
    lane = iota((here, width), 1)
    slot_in = lane // (2 * total)
    first = (lane // total) % 2 == 0
    for i in range(tiles):
        cols = slice(i * width, (i + 1) * width)
        local = spec[0, mine, cols].astype(jnp.float32)
        forward = pltpu.roll(local, total, 1)
        backward = pltpu.roll(local, width - total, 1)
        swapped = jnp.where(first, backward, -forward)
        left = []
        for k in range(per_tile):
            for part in (local, swapped):
                left.append(jnp.where(slot_in == k, part, 0.0).astype(jnp.bfloat16))
        block = dot(jnp.concatenate(left, axis=0), spec[0, :, cols], ((1,), (1,)))
        block = block * (1.0 / total)
        for k in range(per_tile):
            for part in range(2):
                at = (k * 2 + part) * here
                vis[i * per_tile + k, part] = block[at : at + here, :]


def per_device(ns, ng, volts, pfb_window, chan_order, delays, antenna_map, pointing):
    here = volts.shape[0]
    th = volts.shape[1] // FRAME
    inputs = delays.shape[1]
    beams = pointing.shape[0]
    slots = NCH // ng
    total = th * ng
    brows = round_up(beams, 16)
    lanes_g = round_up(2 * slots, 128)
    chunk = round_up(2 * slots * th, 128)
    blocks = NCH * 2 * th // BLOCK
    width = max(128, 2 * total)
    per_tile = width // (2 * total)
    tiles = BLOCK // width
    need = BLOCK // (2 * total) * 2 * th
    span = need if need % 128 == 0 else chunk
    outer = ns // 2 if ns % 2 == 0 else ns
    bf16, f32 = jnp.bfloat16, jnp.float32
    vmem = pl.BlockSpec(memory_space=pltpu.VMEM)
    hbm = pl.BlockSpec(memory_space=pltpu.HBM)
    parts = blocks if need % 128 == 0 else 1
    dims = (ns, ng, slots, here, th, inputs, beams)
    dma = pltpu.SemaphoreType.DMA
    gathered, series = pl.pallas_call(
        functools.partial(gather_kernel, dims),
        out_shape=(
            jax.ShapeDtypeStruct((blocks, inputs, BLOCK), bf16),
            jax.ShapeDtypeStruct((th, beams), f32),
        ),
        in_specs=[hbm, hbm, hbm, pl.BlockSpec(memory_space=pltpu.SMEM), hbm, hbm, hbm],
        out_specs=(pl.BlockSpec(memory_space=pl.ANY), vmem),
        scratch_shapes=[
            pltpu.VMEM(volts.shape, bf16),
            pltpu.VMEM(pfb_window.shape, f32),
            pltpu.VMEM((1, NCH), jnp.int32),
            pltpu.VMEM(delays.shape, f32),
            pltpu.VMEM((1, inputs), jnp.int32),
            pltpu.VMEM((1, beams), jnp.int32),
            dma((6,)),
            pltpu.VMEM((here, (TAPS - 1) * FRAME), bf16),
            pltpu.VMEM((FRAME, ng * lanes_g), bf16),
            pltpu.VMEM((th * lanes_g, chunk), bf16),
            pltpu.VMEM((ng * span, BLOCK), bf16),
            pltpu.VMEM((brows, inputs), f32),
            pltpu.VMEM((blocks * tiles, per_tile * 2 * brows, inputs), bf16),
            pltpu.VMEM((ng, here, chunk), bf16),
            pltpu.VMEM((ng, here, chunk), bf16),
            pltpu.VMEM((blocks, inputs, BLOCK), bf16),
            pltpu.VMEM((ng + 1, brows, round_up(total, 128)), f32),
            dma((2,)),
            dma((parts, ng)),
            dma((parts, ng)),
            dma((2, blocks, outer)),
            dma((2, blocks, outer)),
            dma((blocks, outer)),
            dma((blocks, outer)),
            dma((2, blocks)),
            dma((2, blocks)),
            dma((ng,)),
            dma((ng,)),
            dma((blocks,)),
        ],
        compiler_params=pltpu.CompilerParams(
            collective_id=0, has_side_effects=True, vmem_limit_bytes=63 * 1024 * 1024
        ),
    )(
        volts,
        pfb_window,
        chan_order,
        chan_order,
        delays,
        antenna_map,
        pointing,
    )
    vis = pl.pallas_call(
        functools.partial(vis_kernel, here, total, per_tile, tiles),
        grid=(blocks,),
        out_shape=jax.ShapeDtypeStruct((slots, 2, here, inputs), f32),
        in_specs=[pl.BlockSpec((1, inputs, BLOCK), lambda q: (q, 0, 0))],
        out_specs=pl.BlockSpec(
            (slots // blocks, 2, here, inputs), lambda q: (q, 0, 0, 0)
        ),
        compiler_params=pltpu.CompilerParams(vmem_limit_bytes=48 * 1024 * 1024),
    )(gathered)
    return (vis, series.T)


def solution(mesh):
    ns, ng = mesh.shape["sect"], mesh.shape["grp"]
    return jax.shard_map(
        functools.partial(per_device, ns, ng),
        mesh=mesh,
        in_specs=(P("sect", "grp"), P(), P(), P(), P(), P("sect")),
        out_specs=(P("grp", None, "sect", None), P("sect", "grp")),
        check_vma=False,
    )
```
